32 devices in a mesh: take: 4 (over y, x), outer: 4 (over z), inner: 2 (over core).
Axes of the slice: x: 2, y: 2, z: 4, core: 2. Of those that a mesh axis runs over, the one named last changes fastest.
Arguments:
- frames: bfloat16 [16, 4096, 256], P('take', ('outer', 'inner')), may hold values from -6 to 6
- conv_weight: bfloat16 [3, 3, 256, 256], replicated, may hold values from -0.21875 to 0.21875
- conv_bias: float32 [3, 256], replicated, may hold values from -1 to 1
- dilations: int32 [3], replicated, may hold values from 1 to 64, as said below
- head_weight: bfloat16 [256, 128], replicated, may hold values from -0.375 to 0.375
- present: int32 [16, 4096], P('take', ('outer', 'inner')), may hold values 0 or 1
- frame_keep: float32 [16, 4096], P('take', ('outer', 'inner')), may hold values from 0.5 to 1
- channel_params: float32 [3, 64], replicated, may hold values from 0 to 2
- head_cotangent: bfloat16 [16, 4096, 128], P('take', ('outer', 'inner')), may hold values from -6 to 6
Outputs:
- filtered_mean: float32 [16, 64, 4096], P('take', None, ('outer', 'inner'))
- head_grad: float32 [256, 128], replicated
The draws below stay inside these ranges and needn't reach their ends.
Inputs may be any that keep to these rules, and one draw needn't show every extreme that they name: `dilations`: every dilation is 1 to 64; some layer has exactly 64 and another exactly 1.
All inputs are finite; a program needn't handle non-finite values. No bound on the sum of `present` on one device may be relied on, other than what follows from the above.
Results may differ from the reference program's by a relative error of at most 0.0048.
Values may be sent and summed in bfloat16 or wider, within the bound.
A program may use at most 64 MiB of HBM per device.

```python
import jax
import jax.numpy as jnp
from jax import lax

WIDTH = 256
STATE = 64
LAYERS = 3
DMAX = 64
FR_DEV = 512
TAKES = 16
TOTAL = 4096


def draw_frames(key, part):
    shape = (TAKES, TOTAL, WIDTH)
    values = jax.random.truncated_normal(jax.random.fold_in(key, 1), -6.0, 6.0, shape, jnp.float32)
    return values.astype(jnp.bfloat16)


def draw_dilations(key, part):
    values = jax.random.randint(key, (LAYERS,), 1, DMAX + 1)
    order = jax.random.permutation(jax.random.fold_in(key, 1), LAYERS)
    values = values.at[order[0]].set(DMAX)
    values = values.at[order[1]].set(1)
    return values.astype(jnp.int32)


def draw_frame_keep(key, part):
    chance = jax.random.uniform(jax.random.fold_in(key, 1), (TAKES, TOTAL), jnp.float32)
    level = jax.random.uniform(jax.random.fold_in(key, 2), (TAKES, TOTAL), jnp.float32, 0.5, 0.8)
    return jnp.where(chance < 4.0 / TOTAL, level, 1.0).astype(jnp.float32)


def draw_channel_params(key, part):
    pick = jax.random.uniform(jax.random.fold_in(key, 1), (STATE,), jnp.float32)
    fast_share = 0.4
    drift_share = 0.3
    fast = pick < fast_share
    drift = (pick >= fast_share) & (pick < fast_share + drift_share)
    unit = jax.random.uniform(jax.random.fold_in(key, 2), (3, STATE), jnp.float32)
    low_rate = 0.0012
    high_rate = 1.0 / 30.0
    fast_rate = jnp.exp(jnp.log(low_rate) + unit[0] * jnp.log(high_rate / low_rate))
    slow_rate = jnp.exp(jnp.log(0.05 / TOTAL) + unit[0] * jnp.log(4.0))
    fast_noise = fast_rate * fast_rate * (0.3 + 0.7 * unit[1])
    drift_noise = (0.5 + 1.5 * unit[1]) * 2.0 / (float(TOTAL) * float(FR_DEV))
    long_noise = (0.5 + 1.5 * unit[1]) / float(TOTAL) / float(TOTAL)
    scale = 0.5 + 1.5 * unit[2]
    rate = jnp.where(fast, fast_rate, slow_rate)
    noise = jnp.where(fast, fast_noise, jnp.where(drift, drift_noise, long_noise))
    return jnp.stack([rate, noise, scale]).astype(jnp.float32)


def set_ends(entries, key, low, largest):
    longest = entries.shape.index(max(entries.shape))
    spots = []
    for shift in (0, 1):
        where = [jax.random.randint(jax.random.fold_in(key, axis), (), 0, length) for axis, length in enumerate(entries.shape)]
        where[longest] = (where[longest] + shift) % entries.shape[longest]
        spots.append(tuple(where))
    return entries.at[spots[0]].set(low).at[spots[1]].set(largest)


def block_scale(rng, dims, pieces, low, top_value):
    def one(dim, parts):
        heights = jax.random.uniform(jax.random.fold_in(jax.random.fold_in(rng, 6), dim), (parts,), jnp.float32, low / len(pieces), top_value / len(pieces))
        return jnp.repeat(jnp.exp(heights), dims[dim] // parts).reshape((-1,) + (1,) * (len(dims) - dim - 1))

    level = one(*pieces[0])
    for cut in pieces[1:]:
        level = level * one(*cut)
    return level


def normal_values(own_key, extent, spread, limit, cuts=(), kind=jnp.bfloat16):
    values = jax.random.normal(own_key, extent, jnp.float32) * spread
    if len(cuts) > 0:
        values = block_scale(own_key, extent, cuts, -0.22, 0.18) * values
    return jnp.clip(values, min=-limit, max=limit).astype(kind)


def setup_inputs(seed: int = 0) -> dict:
    key_of = jax.random.split(jax.random.key(seed), 10)
    frames = draw_frames(jax.random.fold_in(key_of[9], 71), 0)
    conv_weight = normal_values(key_of[1], (LAYERS, 3, WIDTH, WIDTH), (3 * WIDTH) ** -0.5, 0.21875)
    conv_bias = jnp.clip(jax.random.uniform(key_of[2], (LAYERS, WIDTH), jnp.float32, -1.0, 1.0), -1.0, 1.0)
    dilations = draw_dilations(jax.random.fold_in(key_of[9], 71), 0)
    head_weight = normal_values(key_of[4], (WIDTH, 2 * STATE), WIDTH ** -0.5, 0.375)
    present = set_ends((jax.random.randint(key_of[5], (TAKES, TOTAL), 0, 4) < 3).astype(jnp.int32), jax.random.fold_in(key_of[5], 1), 0, 1)
    frame_keep = draw_frame_keep(jax.random.fold_in(key_of[9], 71), 0)
    channel_params = draw_channel_params(jax.random.fold_in(key_of[9], 71), 0)
    head_cotangent = normal_values(key_of[8], (TAKES, TOTAL, 2 * STATE), 1.0, 6.0, ((0, 4), (1, 8)))
    return dict(frames=frames, conv_weight=conv_weight, conv_bias=conv_bias, dilations=dilations, head_weight=head_weight, present=present, frame_keep=frame_keep, channel_params=channel_params, head_cotangent=head_cotangent)


def combine(early, late):
    a_one, b_one, c_one, e_one, j_one = early
    a_two, b_two, c_two, e_two, j_two = late
    denom = 1.0 + c_one * j_two
    new_a = a_two * a_one / denom
    new_b = a_two * (b_one + c_one * e_two) / denom + b_two
    new_c = a_two * a_two * c_one / denom + c_two
    new_e = a_one * (e_two - j_two * b_one) / denom + e_one
    new_j = a_one * a_one * j_two / denom + j_one
    return (new_a, new_b, new_c, new_e, new_j)


def doubling_prefix(elems, axis):
    length = elems[0].shape[axis]
    result = elems
    offset = 1
    while offset < length:
        moved = []
        for index, item in enumerate(result):
            fill_value = 1.0 if index == 0 else 0.0
            pad_shape = list(item.shape)
            pad_shape[axis] = offset
            fill = jnp.full(pad_shape, fill_value, item.dtype)
            kept = lax.slice_in_dim(item, 0, length - offset, axis=axis)
            moved.append(jnp.concatenate([fill, kept], axis=axis))
        result = combine(tuple(moved), result)
        offset = offset * 2
    return result


def elements(obs, logp, params, present, keep, first):
    rate = params[0][:, None]
    noise = params[1][:, None]
    scale = params[2][:, None]
    trans = jnp.exp(-rate) * keep
    prec = present * scale * jax.nn.softplus(logp)
    denom = 1.0 + noise * prec
    zeros = jnp.zeros_like(obs)
    elem_a = jnp.where(first, zeros, trans / denom)
    elem_b = jnp.where(first, prec * obs / (1.0 + prec), noise * prec * obs / denom)
    elem_c = jnp.where(first, 1.0 / (1.0 + prec), noise / denom)
    elem_e = jnp.where(first, zeros, trans * prec * obs / denom)
    elem_j = jnp.where(first, zeros, trans * trans * prec / denom)
    return (elem_a, elem_b, elem_c, elem_e, elem_j)


def one_take(frames, present, keep, cotangent, conv_weight, conv_bias, dilations, head_weight, params):
    hidden = frames
    length = frames.shape[0]
    high = lax.Precision.HIGHEST
    for layer in range(LAYERS):
        padded = jnp.pad(hidden.astype(jnp.float32), ((DMAX, DMAX), (0, 0)))
        acc = jnp.zeros((length, WIDTH), jnp.float32)
        for tap in range(3):
            start = (DMAX + (tap - 1) * dilations[layer]).astype(jnp.int32)
            piece = lax.dynamic_slice_in_dim(padded, start, length, 0)
            acc = acc + jnp.dot(piece, conv_weight[layer, tap].astype(jnp.float32), precision=high)
        hidden = (hidden.astype(jnp.float32) + jax.nn.silu(acc + conv_bias[layer][None, :])).astype(jnp.bfloat16)
    hidden_wide = hidden.astype(jnp.float32)
    head = jnp.dot(hidden_wide, head_weight.astype(jnp.float32), precision=high).T
    obs = head[:STATE]
    logp = head[STATE:]
    first = (jnp.arange(length, dtype=jnp.int32) == 0)[None, :]
    elems = elements(obs, logp, params, present.astype(jnp.float32)[None, :], keep[None, :], first)
    result = doubling_prefix(elems, 1)
    grad = jnp.dot(hidden_wide.T, cotangent.astype(jnp.float32), precision=high)
    return result[1], grad


def reference(frames, conv_weight, conv_bias, dilations, head_weight, present, frame_keep, channel_params, head_cotangent):
    means = []
    grad_total = jnp.zeros((WIDTH, 2 * STATE), jnp.float32)
    for index in range(frames.shape[0]):
        mean_one, grad_one = one_take(frames[index], present[index], frame_keep[index], head_cotangent[index], conv_weight, conv_bias, dilations, head_weight, channel_params)
        means.append(mean_one)
        grad_total = grad_total + grad_one
    return jnp.stack(means), grad_total
```

```python
import jax
import jax.numpy as jnp
from jax import lax
from jax.experimental import pallas as pl
from jax.experimental.pallas import tpu as pltpu
from jax.sharding import PartitionSpec as P

STATE = 64
WIDTH = 256
LAYERS = 3
DMAX = 64
HALO = 144
PAD = 192
LANES = 128
MESH = pl.DeviceIdType.MESH
F32 = jnp.float32
BF16 = jnp.bfloat16


def recip(x):
    guess = pl.reciprocal(x, approx=True)
    return guess * (2.0 - x * guess)


def combine(early, late):
    a_one, b_one, c_one, e_one, j_one = early
    a_two, b_two, c_two, e_two, j_two = late
    inv = recip(1.0 + c_one * j_two)
    a_inv = a_two * inv
    back = a_one * inv
    return (
        a_inv * a_one,
        a_inv * (b_one + c_one * e_two) + b_two,
        a_two * a_inv * c_one + c_two,
        back * (e_two - j_two * b_one) + e_one,
        a_one * back * j_two + j_one,
    )


def apply(mean, cov, late):
    a_two, b_two, c_two, e_two, j_two = late
    inv = recip(1.0 + cov * j_two)
    a_inv = a_two * inv
    return a_inv * (mean + cov * e_two) + b_two, a_two * a_inv * cov + c_two


def make_kernel(sizes, takes, block):
    n_take, n_outer, n_inner = sizes
    n_time = n_outer * n_inner
    n_plane = n_take * n_inner
    chunk = WIDTH // n_plane
    pairs = takes // 2
    span = block // 8
    groups = span // 8
    rows = block + 2 * PAD

    def kernel(
        dil, frames, weight, bias, head_w, present, keep, params, cot,
        out, grad_out,
        stage, edge, wv, cv, h0, h1, h2, h3, hw2, pk,
        y_s, r_s, f_s, m_s, tot, grad, g_in, g_mid, g_fin,
        load_sem, halo_send, halo_recv, tot_send, tot_recv,
        a_send, a_recv, b_send, b_recv, c_send, c_recv,
    ):
        take = lax.axis_index("take")
        outer = lax.axis_index("outer")
        inner = lax.axis_index("inner")
        pos = outer * n_inner + inner
        mine = take * n_inner + inner

        def time_id(p):
            return {"outer": p // n_inner, "inner": p % n_inner}

        def plane_id(p):
            return {"take": p // n_inner, "inner": p % n_inner}

        def each(count, body):
            def step(j, carry):
                body(j)
                return carry

            lax.fori_loop(1, count, step, 0)

        barrier = pltpu.get_barrier_semaphore()
        each(n_time, lambda j: pl.semaphore_signal(
            barrier, inc=1, device_id=time_id((pos + j) % n_time), device_id_type=MESH))
        each(n_plane, lambda j: pl.semaphore_signal(
            barrier, inc=1, device_id=plane_id((mine + j) % n_plane), device_id_type=MESH))

        loads = [
            pltpu.make_async_copy(frames, stage, load_sem.at[0]),
            pltpu.make_async_copy(weight.at[0], wv.at[0], load_sem.at[1]),
            pltpu.make_async_copy(weight.at[1], wv.at[1], load_sem.at[2]),
            pltpu.make_async_copy(weight.at[2], wv.at[2], load_sem.at[3]),
            pltpu.make_async_copy(cot, cv, load_sem.at[4]),
        ]
        for load in loads:
            load.start()

        pl.semaphore_wait(barrier, n_time - 1 + n_plane - 1)

        to_late = pltpu.make_async_remote_copy(
            src_ref=frames.at[:, pl.ds(block - HALO, HALO), :], dst_ref=edge.at[0],
            send_sem=halo_send.at[0], recv_sem=halo_recv.at[0],
            device_id=time_id(lax.rem(pos + 1, n_time)), device_id_type=MESH)
        to_early = pltpu.make_async_remote_copy(
            src_ref=frames.at[:, pl.ds(0, HALO), :], dst_ref=edge.at[1],
            send_sem=halo_send.at[1], recv_sem=halo_recv.at[1],
            device_id=time_id(lax.rem(pos + n_time - 1, n_time)), device_id_type=MESH)
        has_early = pos > 0
        has_late = pos < n_time - 1

        @pl.when(has_late)
        def _():
            to_late.start()

        @pl.when(has_early)
        def _():
            to_early.start()

        lane_row = lax.broadcasted_iota(jnp.int32, (2 * STATE, 4 * STATE), 0)
        lane_col = lax.broadcasted_iota(jnp.int32, (2 * STATE, 4 * STATE), 1)
        for part in range(2):
            goal = jnp.where(lane_row < STATE, lane_row, lane_row + STATE) + part * STATE
            pick = jnp.where(lane_col == goal, 1.0, 0.0).astype(BF16)
            hw2[part * WIDTH:(part + 1) * WIDTH, :] = jnp.dot(
                head_w[...], pick, preferred_element_type=F32).astype(BF16)
        par_row = lax.broadcasted_iota(jnp.int32, (STATE, LANES), 0)
        par_col = lax.broadcasted_iota(jnp.int32, (STATE, LANES), 1)
        twice = jnp.where(par_col % STATE == par_row, 1.0, 0.0).astype(F32)
        par = jnp.dot(params[...], twice, precision=lax.Precision.HIGHEST, preferred_element_type=F32)
        decay = jnp.exp(-par[0:1, :])
        noise = jnp.broadcast_to(par[1:2, :], (8, LANES))
        scale = par[2:3, :]

        pk[0:takes, :] = keep[...]
        pk[takes:2 * takes, :] = present[...].astype(F32)
        sel_row = lax.broadcasted_iota(jnp.int32, (2 * takes, LANES), 0)
        sel_col = lax.broadcasted_iota(jnp.int32, (2 * takes, LANES), 1)
        frame_row = lax.broadcasted_iota(jnp.int32, (block, LANES), 0)
        start = (frame_row == 0) & (pos == 0)
        for p in range(pairs):
            which = 2 * p + sel_col // STATE
            for base, dest in ((0, f_s), (takes, r_s)):
                pick = jnp.where(sel_row == base + which, 1.0, 0.0).astype(F32)
                wide = lax.dot_general(
                    pk[...], pick, (((0,), (0,)), ((), ())),
                    precision=lax.Precision.HIGHEST, preferred_element_type=F32)
                if base == 0:
                    dest[p] = jnp.where(start, 0.0, wide * decay)
                else:
                    dest[p] = wide * scale

        loads[0].wait()
        for t in range(takes):
            for half in range(2):
                cols = slice(half * LANES, (half + 1) * LANES)
                h0[half, t, PAD:PAD + block, :] = stage[t, :, cols].astype(F32)
                blank = jnp.zeros((PAD - HALO, LANES), F32)
                h0[half, t, 0:PAD - HALO, :] = blank
                h0[half, t, rows - PAD + HALO:rows, :] = blank

        def conv(layer, src, dst, low, high):
            d = dil[layer]
            size = high - low

            def one(t, carry):
                pieces = []
                for tap in range(3):
                    first = PAD + low + (tap - 1) * d if tap != 1 else PAD + low
                    for half in range(2):
                        pieces.append(src[half, t, pl.ds(first, size), :].astype(BF16))
                acc = jnp.dot(
                    jnp.concatenate(pieces, axis=1), wv[layer], preferred_element_type=F32)
                for half in range(2):
                    cols = slice(half * LANES, (half + 1) * LANES)
                    z = 0.5 * (acc[:, cols] + bias[layer:layer + 1, cols])
                    value = src[half, t, PAD + low:PAD + high, :] + (z + z * jnp.tanh(z))
                    value = value.astype(BF16)
                    if layer == LAYERS - 1:
                        dst[t, low:high, cols] = value
                    else:
                        value = value.astype(F32)
                        before, after = max(0, -low), max(0, high - block)
                        if before:
                            dst[half, t, PAD + low:PAD, :] = jnp.where(
                                has_early, value[:before], 0.0)
                        dst[half, t, PAD + low + before:PAD + high - after, :] = value[before:size - after]
                        if after:
                            dst[half, t, PAD + block:PAD + high, :] = jnp.where(
                                has_late, value[size - after:], 0.0)
                return carry

            lax.fori_loop(0, takes, one, 0)

        inside = (DMAX, 2 * DMAX, 3 * DMAX)
        chain = ((h0, h1), (h1, h2), (h2, h3))
        for layer in range(LAYERS):
            loads[1 + layer].wait()
            conv(layer, *chain[layer], inside[layer], block - inside[layer])

        @pl.when(has_early)
        def _():
            to_late.wait_recv()

        @pl.when(has_late)
        def _():
            to_early.wait_recv()

        for t in range(takes):
            for half in range(2):
                cols = slice(half * LANES, (half + 1) * LANES)
                h0[half, t, PAD - HALO:PAD, :] = jnp.where(
                    has_early, edge[0, t, :, cols].astype(F32), 0.0)
                h0[half, t, PAD + block:PAD + block + HALO, :] = jnp.where(
                    has_late, edge[1, t, :, cols].astype(F32), 0.0)
        reach = (2 * DMAX, DMAX, 0)
        for layer in range(LAYERS):
            conv(layer, *chain[layer], -reach[layer], inside[layer])
            conv(layer, *chain[layer], block - inside[layer], block + reach[layer])

        loads[4].wait()
        term = jnp.zeros((WIDTH, 2 * STATE), F32)
        for t in range(takes):
            term = term + lax.dot_general(
                h3[t], cv[t], (((0,), (0,)), ((), ())), preferred_element_type=F32)
        grad[...] = term.reshape(n_plane, chunk, 2 * STATE)

        def a_copy(target, slot, j):
            return pltpu.make_async_remote_copy(
                src_ref=grad.at[target], dst_ref=g_in.at[slot],
                send_sem=a_send.at[j], recv_sem=a_recv.at[slot],
                device_id=plane_id(target), device_id_type=MESH)

        each(n_plane, lambda j: a_copy((mine + j) % n_plane, mine, j).start())

        for p in range(pairs):
            both = jnp.concatenate([h3[2 * p], h3[2 * p + 1]], axis=1)
            head = jnp.dot(both, hw2[...], preferred_element_type=F32)
            y_s[p] = head[:, :LANES]
            logp = head[:, LANES:]
            soft = jnp.maximum(logp, 0.0) + jnp.log1p(jnp.exp(-jnp.abs(logp)))
            r_s[p] = r_s[p] * soft

        sub = lax.broadcasted_iota(jnp.int32, (8, LANES), 0)
        noise_first = jnp.where((sub == 0) & (pos == 0), 1.0, noise)

        def fields(p, g, i):
            where = pl.ds(g * 8 + i, 8, stride=span)
            q = noise_first if (g == 0 and i == 0) else noise
            return y_s.at[p][where, :], r_s.at[p][where, :], f_s.at[p][where, :], q

        tot[pos] = jnp.zeros((16, LANES), F32)
        prefixes, lasts = [], []
        for p in range(pairs):
            chunks = []
            for g in range(groups):
                a = jnp.ones((8, LANES), F32)
                b = c = e = jj = jnp.zeros((8, LANES), F32)
                for i in range(8):
                    y, r, f, q = fields(p, g, i)
                    a_p = f * a
                    c_p = f * f * c + q
                    b_p = f * b
                    inv = recip(1.0 + r * c_p)
                    gain = r * inv
                    push = gain * (y - b_p)
                    a = a_p * inv
                    c = c_p * inv
                    b = b_p + c_p * push
                    e = e + a_p * push
                    jj = jj + a_p * (a_p * gain)
                chunks.append((a, b, c, e, jj))
            width = 1
            while width < groups:
                for g in range(groups):
                    if g & width:
                        chunks[g] = combine(chunks[(g // width) * width - 1], chunks[g])
                width *= 2
            whole = chunks[groups - 1]
            width = 1
            while width < 8:
                moved = tuple(
                    jnp.where(sub >= width, pltpu.roll(x, width, 0), 1.0 if k == 0 else 0.0)
                    for k, x in enumerate(whole))
                whole = combine(moved, whole)
                width *= 2
            for k in range(5):
                tot[pos, pl.ds(2 * k + p, 1), :] = whole[k][7:8, :]
            lasts.append(tuple(
                jnp.where(sub >= 1, pltpu.roll(x, 1, 0), 1.0 if k == 0 else 0.0)
                for k, x in enumerate(whole)))
            prefixes.append(chunks)

        def t_copy(target, slot, j):
            return pltpu.make_async_remote_copy(
                src_ref=tot.at[slot], dst_ref=tot.at[slot],
                send_sem=tot_send.at[j], recv_sem=tot_recv.at[slot],
                device_id=time_id(target), device_id_type=MESH)

        each(n_time, lambda j: t_copy((pos + j) % n_time, pos, j).start())

        each(n_plane, lambda j: a_copy(mine, (mine + j) % n_plane, j).wait_recv())
        g_in[mine] = grad[mine]
        share = lax.fori_loop(
            1, n_plane, lambda j, s: s + g_in[j], g_in[0])
        g_mid[outer] = share

        def b_copy(target, slot, j):
            return pltpu.make_async_remote_copy(
                src_ref=g_mid.at[slot], dst_ref=g_mid.at[slot],
                send_sem=b_send.at[j], recv_sem=b_recv.at[slot],
                device_id={"outer": target}, device_id_type=MESH)

        each(n_outer, lambda j: b_copy((outer + j) % n_outer, outer, j).start())

        each(n_time, lambda j: t_copy(pos, (pos + j) % n_time, j).wait_recv())

        def pass_on(k, state):
            late = tuple(tot[k, 2 * f:2 * f + 2, :] for f in range(5))
            mean, cov = apply(*state, late)
            return jnp.where(k < pos, mean, state[0]), jnp.where(k < pos, cov, state[1])

        none = jnp.zeros((2, LANES), F32)
        mean, cov = lax.fori_loop(0, n_time - 1, pass_on, (none, none))

        def second(p):
            m_s0 = jnp.broadcast_to(mean[p:p + 1, :], (8, LANES))
            c_s0 = jnp.broadcast_to(cov[p:p + 1, :], (8, LANES))
            m_b, c_b = apply(m_s0, c_s0, lasts[p])
            for g in range(groups):
                m, c = (m_b, c_b) if g == 0 else apply(m_b, c_b, prefixes[p][g - 1])
                for i in range(8):
                    y, r, f, q = fields(p, g, i)
                    c_p = f * f * c + q
                    m_p = f * m
                    c = c_p * recip(1.0 + r * c_p)
                    m = m_p + (c * r) * (y - m_p)
                    m_s.at[p][pl.ds(g * 8 + i, 8, stride=span), :] = m
            flat = m_s[p].T
            out[2 * p] = flat[:STATE]
            out[2 * p + 1] = flat[STATE:]

        second(0)

        each(n_outer, lambda j: b_copy(outer, (outer + j) % n_outer, j).wait_recv())
        g_fin[mine] = lax.fori_loop(1, n_outer, lambda j, s: s + g_mid[j], g_mid[0])

        def c_copy(target, slot, j):
            return pltpu.make_async_remote_copy(
                src_ref=g_fin.at[slot], dst_ref=g_fin.at[slot],
                send_sem=c_send.at[j], recv_sem=c_recv.at[slot],
                device_id=plane_id(target), device_id_type=MESH)

        each(n_plane, lambda j: c_copy((mine + j) % n_plane, mine, j).start())

        for p in range(1, pairs):
            second(p)

        each(n_plane, lambda j: c_copy(mine, (mine + j) % n_plane, j).wait_recv())
        grad_out[...] = g_fin[...].reshape(WIDTH, 2 * STATE)

        @pl.when(has_late)
        def _():
            to_late.wait_send()

        @pl.when(has_early)
        def _():
            to_early.wait_send()

        each(n_plane, lambda j: a_copy((mine + j) % n_plane, mine, j).wait_send())
        each(n_time, lambda j: t_copy((pos + j) % n_time, pos, j).wait_send())
        each(n_outer, lambda j: b_copy((outer + j) % n_outer, outer, j).wait_send())
        each(n_plane, lambda j: c_copy((mine + j) % n_plane, mine, j).wait_send())

    vmem = pl.BlockSpec(memory_space=pltpu.VMEM)
    smem = pl.BlockSpec(memory_space=pltpu.SMEM)
    hbm = pl.BlockSpec(memory_space=pl.ANY)
    dma = pltpu.SemaphoreType.DMA
    return pl.pallas_call(
        kernel,
        out_shape=(
            jax.ShapeDtypeStruct((takes, STATE, block), F32),
            jax.ShapeDtypeStruct((WIDTH, 2 * STATE), F32),
        ),
        in_specs=[smem, hbm, hbm, vmem, vmem, vmem, vmem, vmem, hbm],
        out_specs=(vmem, vmem),
        scratch_shapes=[
            pltpu.VMEM((takes, block, WIDTH), BF16),
            pltpu.VMEM((2, takes, HALO, WIDTH), BF16),
            pltpu.VMEM((LAYERS, 3 * WIDTH, WIDTH), BF16),
            pltpu.VMEM((takes, block, 2 * STATE), BF16),
            pltpu.VMEM((2, takes, rows, LANES), F32),
            pltpu.VMEM((2, takes, rows, LANES), F32),
            pltpu.VMEM((2, takes, rows, LANES), F32),
            pltpu.VMEM((takes, block, WIDTH), BF16),
            pltpu.VMEM((2 * WIDTH, 4 * STATE), BF16),
            pltpu.VMEM((2 * takes, block), F32),
            pltpu.VMEM((pairs, block, LANES), F32),
            pltpu.VMEM((pairs, block, LANES), F32),
            pltpu.VMEM((pairs, block, LANES), F32),
            pltpu.VMEM((pairs, block, LANES), F32),
            pltpu.VMEM((n_time, 16, LANES), F32),
            pltpu.VMEM((n_plane, chunk, 2 * STATE), F32),
            pltpu.VMEM((n_plane, chunk, 2 * STATE), F32),
            pltpu.VMEM((n_outer, chunk, 2 * STATE), F32),
            pltpu.VMEM((n_plane, chunk, 2 * STATE), F32),
            dma((5,)), dma((2,)), dma((2,)),
            dma((n_time,)), dma((n_time,)),
            dma((n_plane,)), dma((n_plane,)),
            dma((n_outer,)), dma((n_outer,)),
            dma((n_plane,)), dma((n_plane,)),
        ],
        compiler_params=pltpu.CompilerParams(
            collective_id=0, has_side_effects=True, vmem_limit_bytes=48 * 1024 * 1024),
        cost_estimate=pl.CostEstimate(
            flops=4 * 1000 * 1000 * 1000, bytes_accessed=4 * 1000 * 1000, transcendentals=0),
    )


def solution(mesh):
    sizes = (mesh.shape["take"], mesh.shape["outer"], mesh.shape["inner"])

    def per_device(
        frames, conv_weight, conv_bias, dilations, head_weight,
        present, frame_keep, channel_params, head_cotangent,
    ):
        takes, block, width = frames.shape
        call = make_kernel(sizes, takes, block)
        return call(
            dilations, frames, conv_weight.reshape(LAYERS, 3 * width, width), conv_bias,
            head_weight, present, frame_keep, channel_params, head_cotangent)

    return jax.shard_map(
        per_device,
        mesh=mesh,
        in_specs=(
            P("take", ("outer", "inner"), None),
            P(),
            P(),
            P(),
            P(),
            P("take", ("outer", "inner")),
            P("take", ("outer", "inner")),
            P(),
            P("take", ("outer", "inner"), None),
        ),
        out_specs=(P("take", None, ("outer", "inner")), P()),
        check_vma=False,
    )
```

```python
import jax
import jax.numpy as jnp
from jax import lax
from jax.experimental import pallas as pl
from jax.experimental.pallas import tpu as pltpu
from jax.sharding import PartitionSpec as P

STATE = 64
WIDTH = 256
LAYERS = 3
DMAX = 64
HALO = 144
PAD = 192
LANES = 128
MESH = pl.DeviceIdType.MESH
F32 = jnp.float32
BF16 = jnp.bfloat16


def recip(x):
    guess = pl.reciprocal(x, approx=True)
    return guess * (2.0 - x * guess)


def combine(early, late):
    a_one, b_one, c_one, e_one, j_one = early
    a_two, b_two, c_two, e_two, j_two = late
    inv = recip(1.0 + c_one * j_two)
    a_inv = a_two * inv
    back = a_one * inv
    return (
        a_inv * a_one,
        a_inv * (b_one + c_one * e_two) + b_two,
        a_two * a_inv * c_one + c_two,
        back * (e_two - j_two * b_one) + e_one,
        a_one * back * j_two + j_one,
    )


def apply(mean, cov, late):
    a_two, b_two, c_two, e_two, j_two = late
    inv = recip(1.0 + cov * j_two)
    a_inv = a_two * inv
    return a_inv * (mean + cov * e_two) + b_two, a_two * a_inv * cov + c_two


def make_kernel(sizes, takes, block):
    n_take, n_outer, n_inner = sizes
    n_time = n_outer * n_inner
    n_plane = n_take * n_inner
    chunk = WIDTH // n_plane
    pairs = takes // 2
    span = block // 8
    groups = span // 8
    rows = block + 2 * PAD

    def kernel(
        dil, frames, weight, bias_in, head_in, present_in, keep_in, params_in, cot,
        out, grad_out,
        bias, head_w, present, keep, params,
        stage, edge, wv, cv, h0, h1, h2, h3, hw2, pk,
        y_s, r_s, f_s, m_s, tot, grad, g_in, g_mid, g_fin,
        load_sem, halo_send, halo_recv, tot_send, tot_recv,
        a_send, a_recv, b_send, b_recv, c_send, c_recv,
    ):
        take = lax.axis_index("take")
        outer = lax.axis_index("outer")
        inner = lax.axis_index("inner")
        pos = outer * n_inner + inner
        mine = take * n_inner + inner

        def time_id(p):
            return {"outer": p // n_inner, "inner": p % n_inner}

        def plane_id(p):
            return {"take": p // n_inner, "inner": p % n_inner}

        def each(count, body):
            def step(j, carry):
                body(j)
                return carry

            lax.fori_loop(1, count, step, 0)

        barrier = pltpu.get_barrier_semaphore()
        each(n_time, lambda j: pl.semaphore_signal(
            barrier, inc=1, device_id=time_id((pos + j) % n_time), device_id_type=MESH))
        each(n_plane, lambda j: pl.semaphore_signal(
            barrier, inc=1, device_id=plane_id((mine + j) % n_plane), device_id_type=MESH))

        loads = [
            pltpu.make_async_copy(frames, stage, load_sem.at[0]),
            pltpu.make_async_copy(weight.at[0], wv.at[0], load_sem.at[1]),
            pltpu.make_async_copy(weight.at[1], wv.at[1], load_sem.at[2]),
            pltpu.make_async_copy(weight.at[2], wv.at[2], load_sem.at[3]),
            pltpu.make_async_copy(cot, cv, load_sem.at[4]),
        ]
        small = [
            pltpu.make_async_copy(source, target, load_sem.at[5 + k])
            for k, (source, target) in enumerate((
                (bias_in, bias), (head_in, head_w), (present_in, present),
                (keep_in, keep), (params_in, params)))
        ]
        for load in small:
            load.start()
        for load in loads:
            load.start()

        pl.semaphore_wait(barrier, n_time - 1 + n_plane - 1)

        to_late = pltpu.make_async_remote_copy(
            src_ref=frames.at[:, pl.ds(block - HALO, HALO), :], dst_ref=edge.at[0],
            send_sem=halo_send.at[0], recv_sem=halo_recv.at[0],
            device_id=time_id(lax.rem(pos + 1, n_time)), device_id_type=MESH)
        to_early = pltpu.make_async_remote_copy(
            src_ref=frames.at[:, pl.ds(0, HALO), :], dst_ref=edge.at[1],
            send_sem=halo_send.at[1], recv_sem=halo_recv.at[1],
            device_id=time_id(lax.rem(pos + n_time - 1, n_time)), device_id_type=MESH)
        has_early = pos > 0
        has_late = pos < n_time - 1

        @pl.when(has_late)
        def _():
            to_late.start()

        @pl.when(has_early)
        def _():
            to_early.start()

        for load in small:
            load.wait()
        lane_row = lax.broadcasted_iota(jnp.int32, (2 * STATE, 4 * STATE), 0)
        lane_col = lax.broadcasted_iota(jnp.int32, (2 * STATE, 4 * STATE), 1)
        for part in range(2):
            goal = jnp.where(lane_row < STATE, lane_row, lane_row + STATE) + part * STATE
            pick = jnp.where(lane_col == goal, 1.0, 0.0).astype(BF16)
            hw2[part * WIDTH:(part + 1) * WIDTH, :] = jnp.dot(
                head_w[...], pick, preferred_element_type=F32).astype(BF16)
        par_row = lax.broadcasted_iota(jnp.int32, (STATE, LANES), 0)
        par_col = lax.broadcasted_iota(jnp.int32, (STATE, LANES), 1)
        twice = jnp.where(par_col % STATE == par_row, 1.0, 0.0).astype(F32)
        par = jnp.dot(params[...], twice, precision=lax.Precision.HIGHEST, preferred_element_type=F32)
        decay = jnp.exp(-par[0:1, :])
        noise = jnp.broadcast_to(par[1:2, :], (8, LANES))
        scale = par[2:3, :]

        left = keep[...]
        for k in range(3):
            term = left.astype(BF16).astype(F32)
            pk[k * takes:(k + 1) * takes, :] = term
            left = left - term
        pk[3 * takes:4 * takes, :] = present[...].astype(F32)
        sel_row = lax.broadcasted_iota(jnp.int32, (4 * takes, 2 * pairs * LANES), 0)
        sel_col = lax.broadcasted_iota(jnp.int32, (4 * takes, 2 * pairs * LANES), 1)
        same = sel_row % takes == sel_col // STATE % takes
        is_keep = (sel_row < 3 * takes) == (sel_col < pairs * LANES)
        pick = jnp.where(same & is_keep, 1.0, 0.0).astype(BF16)
        wide = lax.dot_general(
            pk[...].astype(BF16), pick, (((0,), (0,)), ((), ())), preferred_element_type=F32)
        frame_row = lax.broadcasted_iota(jnp.int32, (block, LANES), 0)
        start = (frame_row == 0) & (pos == 0)
        for p in range(pairs):
            f_s[p] = jnp.where(start, 0.0, wide[:, p * LANES:(p + 1) * LANES] * decay)
            r_s[p] = wide[:, (pairs + p) * LANES:(pairs + p + 1) * LANES] * scale

        loads[0].wait()
        for t in range(takes):
            for half in range(2):
                cols = slice(half * LANES, (half + 1) * LANES)
                h0[half, t, PAD:PAD + block, :] = stage[t, :, cols].astype(F32)
                blank = jnp.zeros((PAD - HALO, LANES), F32)
                h0[half, t, 0:PAD - HALO, :] = blank
                h0[half, t, rows - PAD + HALO:rows, :] = blank

        def conv(layer, src, dst, spans):
            d = dil[layer]

            def one(duo, carry):
                parts = [(2 * duo + k, low, high) for k in range(2) for low, high in spans]
                inputs = []
                for t, low, high in parts:
                    pieces = []
                    for tap in range(3):
                        first = PAD + low + (tap - 1) * d if tap != 1 else PAD + low
                        for half in range(2):
                            pieces.append(src[half, t, pl.ds(first, high - low), :].astype(BF16))
                    inputs.append(jnp.concatenate(pieces, axis=1))
                total = jnp.dot(
                    jnp.concatenate(inputs, axis=0), wv[layer], preferred_element_type=F32)
                taken = 0
                for t, low, high in parts:
                    size = high - low
                    acc = total[taken:taken + size]
                    taken += size
                    for half in range(2):
                        cols = slice(half * LANES, (half + 1) * LANES)
                        z = 0.5 * (acc[:, cols] + bias[layer:layer + 1, cols])
                        value = src[half, t, PAD + low:PAD + high, :] + (z + z * jnp.tanh(z))
                        value = value.astype(BF16)
                        if layer == LAYERS - 1:
                            dst[t, low:high, cols] = value
                        else:
                            value = value.astype(F32)
                            before, after = max(0, -low), max(0, high - block)
                            if before:
                                dst[half, t, PAD + low:PAD, :] = jnp.where(
                                    has_early, value[:before], 0.0)
                            dst[half, t, PAD + low + before:PAD + high - after, :] = value[before:size - after]
                            if after:
                                dst[half, t, PAD + block:PAD + high, :] = jnp.where(
                                    has_late, value[size - after:], 0.0)
                return carry

            lax.fori_loop(0, takes // 2, one, 0)

        loads[1].wait()
        conv(0, h0, h1, [(DMAX, block - DMAX)])
        loads[2].wait()
        conv(1, h1, h2, [(2 * DMAX, block - 2 * DMAX)])

        @pl.when(has_early)
        def _():
            to_late.wait_recv()

        @pl.when(has_late)
        def _():
            to_early.wait_recv()

        for t in range(takes):
            for half in range(2):
                cols = slice(half * LANES, (half + 1) * LANES)
                h0[half, t, PAD - HALO:PAD, :] = jnp.where(
                    has_early, edge[0, t, :, cols].astype(F32), 0.0)
                h0[half, t, PAD + block:PAD + block + HALO, :] = jnp.where(
                    has_late, edge[1, t, :, cols].astype(F32), 0.0)
        conv(0, h0, h1, [(-2 * DMAX, DMAX), (block - DMAX, block + 2 * DMAX)])
        conv(1, h1, h2, [(-DMAX, 2 * DMAX), (block - 2 * DMAX, block + DMAX)])
        loads[3].wait()
        conv(2, h2, h3, [(0, block)])

        loads[4].wait()
        term = jnp.zeros((WIDTH, 2 * STATE), F32)
        for t in range(takes):
            term = term + lax.dot_general(
                h3[t], cv[t], (((0,), (0,)), ((), ())), preferred_element_type=F32)
        grad[...] = term.reshape(n_plane, chunk, 2 * STATE)

        def a_copy(target, slot, j):
            return pltpu.make_async_remote_copy(
                src_ref=grad.at[target], dst_ref=g_in.at[slot],
                send_sem=a_send.at[j], recv_sem=a_recv.at[slot],
                device_id=plane_id(target), device_id_type=MESH)

        each(n_plane, lambda j: a_copy((mine + j) % n_plane, mine, j).start())

        for p in range(pairs):
            both = jnp.concatenate([h3[2 * p], h3[2 * p + 1]], axis=1)
            head = jnp.dot(both, hw2[...], preferred_element_type=F32)
            y_s[p] = head[:, :LANES]
            logp = head[:, LANES:]
            soft = jnp.maximum(logp, 0.0) + jnp.log1p(jnp.exp(-jnp.abs(logp)))
            r_s[p] = r_s[p] * soft

        sub = lax.broadcasted_iota(jnp.int32, (8, LANES), 0)
        noise_first = jnp.where((sub == 0) & (pos == 0), 1.0, noise)

        def fields(p, g, i):
            where = pl.ds(g * 8 + i, 8, stride=span)
            q = noise_first if (g == 0 and i == 0) else noise
            return y_s.at[p][where, :], r_s.at[p][where, :], f_s.at[p][where, :], q

        tot[pos] = jnp.zeros((16, LANES), F32)
        prefixes, lasts = [], []
        for p in range(pairs):
            chunks = []
            for g in range(groups):
                a = jnp.ones((8, LANES), F32)
                b = c = e = jj = jnp.zeros((8, LANES), F32)
                for i in range(8):
                    y, r, f, q = fields(p, g, i)
                    a_p = f * a
                    c_p = f * f * c + q
                    b_p = f * b
                    inv = recip(1.0 + r * c_p)
                    gain = r * inv
                    push = gain * (y - b_p)
                    a = a_p * inv
                    c = c_p * inv
                    b = b_p + c_p * push
                    e = e + a_p * push
                    jj = jj + a_p * (a_p * gain)
                chunks.append((a, b, c, e, jj))
            width = 1
            while width < groups:
                for g in range(groups):
                    if g & width:
                        chunks[g] = combine(chunks[(g // width) * width - 1], chunks[g])
                width *= 2
            whole = chunks[groups - 1]
            width = 1
            while width < 8:
                moved = tuple(
                    jnp.where(sub >= width, pltpu.roll(x, width, 0), 1.0 if k == 0 else 0.0)
                    for k, x in enumerate(whole))
                whole = combine(moved, whole)
                width *= 2
            for k in range(5):
                tot[pos, pl.ds(2 * k + p, 1), :] = whole[k][7:8, :]
            lasts.append(tuple(
                jnp.where(sub >= 1, pltpu.roll(x, 1, 0), 1.0 if k == 0 else 0.0)
                for k, x in enumerate(whole)))
            prefixes.append(chunks)

        def t_copy(target, slot, j):
            return pltpu.make_async_remote_copy(
                src_ref=tot.at[slot], dst_ref=tot.at[slot],
                send_sem=tot_send.at[j], recv_sem=tot_recv.at[slot],
                device_id=time_id(target), device_id_type=MESH)

        each(n_time, lambda j: t_copy((pos + j) % n_time, pos, j).start())

        each(n_plane, lambda j: a_copy(mine, (mine + j) % n_plane, j).wait_recv())
        g_in[mine] = grad[mine]
        share = lax.fori_loop(
            1, n_plane, lambda j, s: s + g_in[j], g_in[0])
        g_mid[outer] = share

        def b_copy(target, slot, j):
            return pltpu.make_async_remote_copy(
                src_ref=g_mid.at[slot], dst_ref=g_mid.at[slot],
                send_sem=b_send.at[j], recv_sem=b_recv.at[slot],
                device_id={"outer": target}, device_id_type=MESH)

        each(n_outer, lambda j: b_copy((outer + j) % n_outer, outer, j).start())

        each(n_time, lambda j: t_copy(pos, (pos + j) % n_time, j).wait_recv())

        def pass_on(k, state):
            late = tuple(tot[k, 2 * f:2 * f + 2, :] for f in range(5))
            mean, cov = apply(*state, late)
            return jnp.where(k < pos, mean, state[0]), jnp.where(k < pos, cov, state[1])

        none = jnp.zeros((2, LANES), F32)
        mean, cov = lax.fori_loop(0, n_time - 1, pass_on, (none, none))

        def second(p):
            m_s0 = jnp.broadcast_to(mean[p:p + 1, :], (8, LANES))
            c_s0 = jnp.broadcast_to(cov[p:p + 1, :], (8, LANES))
            m_b, c_b = apply(m_s0, c_s0, lasts[p])
            for g in range(groups):
                m, c = (m_b, c_b) if g == 0 else apply(m_b, c_b, prefixes[p][g - 1])
                for i in range(8):
                    y, r, f, q = fields(p, g, i)
                    c_p = f * f * c + q
                    m_p = f * m
                    c = c_p * recip(1.0 + r * c_p)
                    m = m_p + (c * r) * (y - m_p)
                    m_s.at[p][pl.ds(g * 8 + i, 8, stride=span), :] = m
            flat = m_s[p].T
            out[2 * p] = flat[:STATE]
            out[2 * p + 1] = flat[STATE:]

        second(0)

        each(n_outer, lambda j: b_copy(outer, (outer + j) % n_outer, j).wait_recv())
        g_fin[mine] = lax.fori_loop(1, n_outer, lambda j, s: s + g_mid[j], g_mid[0])

        def c_copy(target, slot, j):
            return pltpu.make_async_remote_copy(
                src_ref=g_fin.at[slot], dst_ref=g_fin.at[slot],
                send_sem=c_send.at[j], recv_sem=c_recv.at[slot],
                device_id=plane_id(target), device_id_type=MESH)

        each(n_plane, lambda j: c_copy((mine + j) % n_plane, mine, j).start())

        for p in range(1, pairs):
            second(p)

        each(n_plane, lambda j: c_copy(mine, (mine + j) % n_plane, j).wait_recv())
        grad_out[...] = g_fin[...].reshape(WIDTH, 2 * STATE)

        @pl.when(has_late)
        def _():
            to_late.wait_send()

        @pl.when(has_early)
        def _():
            to_early.wait_send()

        each(n_plane, lambda j: a_copy((mine + j) % n_plane, mine, j).wait_send())
        each(n_time, lambda j: t_copy((pos + j) % n_time, pos, j).wait_send())
        each(n_outer, lambda j: b_copy((outer + j) % n_outer, outer, j).wait_send())
        each(n_plane, lambda j: c_copy((mine + j) % n_plane, mine, j).wait_send())

    vmem = pl.BlockSpec(memory_space=pltpu.VMEM)
    smem = pl.BlockSpec(memory_space=pltpu.SMEM)
    hbm = pl.BlockSpec(memory_space=pl.ANY)
    dma = pltpu.SemaphoreType.DMA
    return pl.pallas_call(
        kernel,
        out_shape=(
            jax.ShapeDtypeStruct((takes, STATE, block), F32),
            jax.ShapeDtypeStruct((WIDTH, 2 * STATE), F32),
        ),
        in_specs=[smem] + [hbm] * 8,
        out_specs=(vmem, vmem),
        scratch_shapes=[
            pltpu.VMEM((LAYERS, WIDTH), F32),
            pltpu.VMEM((WIDTH, 2 * STATE), BF16),
            pltpu.VMEM((takes, block), jnp.int32),
            pltpu.VMEM((takes, block), F32),
            pltpu.VMEM((3, STATE), F32),
            pltpu.VMEM((takes, block, WIDTH), BF16),
            pltpu.VMEM((2, takes, HALO, WIDTH), BF16),
            pltpu.VMEM((LAYERS, 3 * WIDTH, WIDTH), BF16),
            pltpu.VMEM((takes, block, 2 * STATE), BF16),
            pltpu.VMEM((2, takes, rows, LANES), F32),
            pltpu.VMEM((2, takes, rows, LANES), F32),
            pltpu.VMEM((2, takes, rows, LANES), F32),
            pltpu.VMEM((takes, block, WIDTH), BF16),
            pltpu.VMEM((2 * WIDTH, 4 * STATE), BF16),
            pltpu.VMEM((4 * takes, block), F32),
            pltpu.VMEM((pairs, block, LANES), F32),
            pltpu.VMEM((pairs, block, LANES), F32),
            pltpu.VMEM((pairs, block, LANES), F32),
            pltpu.VMEM((pairs, block, LANES), F32),
            pltpu.VMEM((n_time, 16, LANES), F32),
            pltpu.VMEM((n_plane, chunk, 2 * STATE), F32),
            pltpu.VMEM((n_plane, chunk, 2 * STATE), F32),
            pltpu.VMEM((n_outer, chunk, 2 * STATE), F32),
            pltpu.VMEM((n_plane, chunk, 2 * STATE), F32),
            dma((10,)), dma((2,)), dma((2,)),
            dma((n_time,)), dma((n_time,)),
            dma((n_plane,)), dma((n_plane,)),
            dma((n_outer,)), dma((n_outer,)),
            dma((n_plane,)), dma((n_plane,)),
        ],
        compiler_params=pltpu.CompilerParams(
            collective_id=0, has_side_effects=True, vmem_limit_bytes=62 * 1024 * 1024),
        cost_estimate=pl.CostEstimate(
            flops=4 * 1000 * 1000 * 1000, bytes_accessed=4 * 1000 * 1000, transcendentals=0),
    )


def solution(mesh):
    sizes = (mesh.shape["take"], mesh.shape["outer"], mesh.shape["inner"])

    def per_device(
        frames, conv_weight, conv_bias, dilations, head_weight,
        present, frame_keep, channel_params, head_cotangent,
    ):
        takes, block, width = frames.shape
        call = make_kernel(sizes, takes, block)
        return call(
            dilations, frames, conv_weight.reshape(LAYERS, 3 * width, width), conv_bias,
            head_weight, present, frame_keep, channel_params, head_cotangent)

    return jax.shard_map(
        per_device,
        mesh=mesh,
        in_specs=(
            P("take", ("outer", "inner"), None),
            P(),
            P(),
            P(),
            P(),
            P("take", ("outer", "inner")),
            P("take", ("outer", "inner")),
            P(),
            P("take", ("outer", "inner"), None),
        ),
        out_specs=(P("take", None, ("outer", "inner")), P()),
        check_vma=False,
    )
```
